256 devices in a mesh: half: 2 (over z_hi), point: 64 (over z_lo, y, x), row: 2 (over core).
Axes of the slice: x: 4, y: 4, z: 8 (z_hi: 2, z_lo: 4; z = z_hi * 4 + z_lo), core: 2. Of those that a mesh axis runs over, the one named last changes fastest.
Arguments:
- children: float32 [2, 2048, 128, 128], P('half', 'point', 'row'), may hold values from -0.0390625 to 0.0390625
- residual_series: float32 [2048, 8192], P('point', ('row', 'half')), may hold values from -0.0390625 to 0.0390625
Outputs:
- basis_values: float32 [2, 2048, 128, 128], P(None, 'point', ('row', 'half'))
- residual_values: float32 [2, 2048, 8192], P(None, 'point', ('row', 'half'))
The draws below stay inside these ranges and needn't reach their ends.
All inputs are finite; a program needn't handle non-finite values.
Results may differ from the reference program's by a relative error of at most 0.0001.
Values sent between devices are 32-bit elements; how exact they have to be, the bound alone decides.
A program may use at most 128 MiB of HBM per device.

```python
import math
import jax
import jax.numpy as jnp
from jax import lax

BASIS = 128
BLOCK = 64
LENGTH = 524288
PT_DEV = 32
POINTS = 2048
N_POINT = 64


def shard_levels(rng, dims, split, least, top_value):
    level, own = 1.0, jax.random.fold_in(rng, 6)
    for axis_at, shards_of in split:
        draws = jnp.exp(jax.random.uniform(jax.random.fold_in(own, axis_at), (shards_of,), jnp.float32, least / len(split), top_value / len(split)))
        level = level * jnp.repeat(draws, dims[axis_at] // shards_of).reshape([-1 if axis == axis_at else 1 for axis in range(len(dims))])
    return level


def scatter_about(rng, extent, spread, reach, split=(), kind=jnp.bfloat16):
    array = spread * jax.random.normal(rng, extent, jnp.float32)
    if split:
        array = array * shard_levels(rng, extent, split, -0.22, 0.18)
    return jnp.clip(array, -reach, reach).astype(kind)


def setup_inputs(seed: int = 0) -> dict:
    keys = jax.random.split(jax.random.key(seed), 3)
    children = scatter_about(keys[0], (2, POINTS, BASIS, BASIS), (11 * POINTS) ** -0.5, 0.0390625, ((0, 2), (1, 64), (2, 2)), jnp.float32)
    residual_series = scatter_about(keys[1], (POINTS, BASIS * BLOCK), (11 * POINTS) ** -0.5, 0.0390625, ((0, 64), (1, 4)), jnp.float32)
    return {"children": children, "residual_series": residual_series}


def rotation(phases):
    wrapped = jnp.bitwise_and(phases, LENGTH - 1)
    radians = wrapped.astype(jnp.float32) * (2.0 * math.pi / LENGTH)
    return jnp.cos(radians), jnp.sin(radians)


def evaluate(series, groups, within):
    entries = series.shape[1]
    stride = LENGTH // (groups * within)
    group_ids = jnp.arange(groups, dtype=jnp.int32)
    inner_ids = jnp.arange(within, dtype=jnp.int32)
    base_step = group_ids * stride + 1
    outer_cos, outer_sin = rotation((group_ids * within)[None, :] * base_step[:, None])
    twist_cos, twist_sin = rotation(inner_ids[None, :] * base_step[:, None])
    inner_cos, inner_sin = rotation(inner_ids[:, None] * inner_ids[None, :] * (LENGTH // within))
    folded = series.reshape(groups, within * entries)
    outer_re = jnp.dot(outer_cos, folded, precision=lax.Precision.HIGHEST, preferred_element_type=jnp.float32).reshape(groups, within, entries)
    outer_im = jnp.dot(outer_sin, folded, precision=lax.Precision.HIGHEST, preferred_element_type=jnp.float32).reshape(groups, within, entries)
    turned_re = outer_re * twist_cos[:, :, None] - outer_im * twist_sin[:, :, None]
    turned_im = outer_re * twist_sin[:, :, None] + outer_im * twist_cos[:, :, None]
    hp = lax.Precision.HIGHEST
    value_re = jnp.einsum("st,qte->qse", inner_cos, turned_re, precision=hp) - jnp.einsum("st,qte->qse", inner_sin, turned_im, precision=hp)
    value_im = jnp.einsum("st,qte->qse", inner_cos, turned_im, precision=hp) + jnp.einsum("st,qte->qse", inner_sin, turned_re, precision=hp)
    return jnp.stack([value_re.reshape(groups * within, entries), value_im.reshape(groups * within, entries)])


def complex_product(left_factor, right_factor):
    hp = lax.Precision.HIGHEST
    real_part = jnp.einsum("cik,ckj->cij", left_factor[0], right_factor[0], precision=hp) - jnp.einsum("cik,ckj->cij", left_factor[1], right_factor[1], precision=hp)
    imag_part = jnp.einsum("cik,ckj->cij", left_factor[0], right_factor[1], precision=hp) + jnp.einsum("cik,ckj->cij", left_factor[1], right_factor[0], precision=hp)
    return jnp.stack([real_part, imag_part])


def reference(children, residual_series):
    lower_values = evaluate(children[0].reshape(POINTS, BASIS * BASIS), N_POINT, PT_DEV).reshape(2, POINTS, BASIS, BASIS)
    upper_values = evaluate(children[1].reshape(POINTS, BASIS * BASIS), N_POINT, PT_DEV).reshape(2, POINTS, BASIS, BASIS)
    series_values = evaluate(residual_series, N_POINT, PT_DEV).reshape(2, POINTS, BASIS, BLOCK)
    basis_values = complex_product(upper_values, lower_values)
    residual_values = complex_product(lower_values, series_values).reshape(2, POINTS, BASIS * BLOCK)
    return (basis_values, residual_values)
```

```python
import math

import jax
import jax.numpy as jnp
import numpy as np
from jax import lax
from jax.experimental import pallas as pl
from jax.experimental.pallas import tpu as pltpu
from jax.sharding import PartitionSpec as P

BASIS = 128
BLOCK = 64
LENGTH = 524288
WITHIN = 32
GROUPS = 64
PLANE = 16
RING = 8
WAVES = 5
HOPS = 5
PARTS = 4
SLAB = PLANE * WITHIN
PART = SLAB // PARTS
MESH = pl.DeviceIdType.MESH
F32 = jnp.float32
BF16 = jnp.bfloat16


def split_matrix(matrix):
    matrix = matrix.astype(np.float32)
    high = matrix.astype(jnp.bfloat16)
    low = (matrix - high.astype(np.float32)).astype(jnp.bfloat16)
    return np.concatenate([high, high, low, low], axis=-1)


def transform_matrices():
    q = np.arange(GROUPS).reshape(4, PLANE)
    p = np.arange(GROUPS)
    phase = (32 * p[None, None, :] * (256 * q[:, :, None] + 1)) % LENGTH
    angle = phase * (2.0 * math.pi / LENGTH)
    outer = np.concatenate([np.cos(angle), np.sin(angle)], axis=1)
    t = np.arange(WITHIN)
    s = np.arange(WITHIN)
    phase = t[None, None, None, :] * (s[None, None, :, None] * 16384 + 256 * q[:, :, None, None] + 1)
    angle = (phase % LENGTH) * (2.0 * math.pi / LENGTH)
    cos, sin = np.cos(angle), np.sin(angle)
    real = np.concatenate([cos, -sin], axis=-1).reshape(4, PLANE, 2, 1, 16, 64)
    imag = np.concatenate([sin, cos], axis=-1).reshape(4, PLANE, 2, 1, 16, 64)
    inner = np.concatenate([real, imag], axis=3).reshape(4, PLANE * 64, 64)
    return split_matrix(outer), split_matrix(inner)


def halves(x):
    high = x.astype(BF16)
    return high, (x - high.astype(F32)).astype(BF16)


def stacked_halves(x):
    high, low = halves(x)
    return jnp.concatenate([high, low, high, low], axis=0)


def dot(a, b):
    return jnp.dot(a, b, preferred_element_type=F32)


def rows(offset, count):
    return pl.ds(pl.multiple_of(offset, 8), count)


def reach(wave, source, direction):
    if wave == 4:
        return 4 if direction == 0 else 3
    lower = source + 2 if direction == 0 else 5 - source
    if wave % 2 == 1:
        upper = 7 - source if direction == 0 else source - 4
    elif direction == 0:
        upper = jnp.where(source >= 6, 11 - source, 0)
    else:
        upper = jnp.where(source <= 5, source, 0)
    return jnp.where(source < 4, lower, upper)


def kernel(
    child, series, outer_all, inner_all, basis_out, residual_out,
    gathered, sending, mid, spectra, received, products, pairs, mixed, lanes, outer, inner,
    a_send, a_recv, own_sem, z_send, z_recv, d_send, d_recv, const_sem, out_local, out_send, out_recv,
):
    half = lax.axis_index("half")
    point = lax.axis_index("point")
    core = lax.axis_index("row")
    z = point // 16
    plane = point % 16
    y = plane // 4
    x = plane % 4
    ring = half * 4 + z

    def plane_peer(i):
        dy, dx = (i // 4) % 4, i % 4
        return ((y + dy) % 4) * 4 + (x + dx) % 4

    def ring_device(position):
        return (position // 4, (position % 4) * 16 + plane, core)

    consts = [
        pltpu.make_async_copy(outer_all.at[z], outer, const_sem.at[0]),
        pltpu.make_async_copy(inner_all.at[z], inner, const_sem.at[1]),
    ]
    for copy in consts:
        copy.start()

    barrier = pltpu.get_barrier_semaphore()

    def greet(i, carry):
        peer = plane_peer(i)
        pl.semaphore_signal(barrier, inc=1, device_id=(half, z * 16 + peer, (core + i // 16) % 2), device_id_type=MESH)
        return carry

    lax.fori_loop(1, 32, greet, 0)
    for step in (1, 7):
        pl.semaphore_signal(barrier, inc=1, device_id=ring_device((ring + step) % 8), device_id_type=MESH)

    for wave in range(WAVES):
        for m in range(PLANE):
            base = (wave * PLANE + m) * WITHIN
            if wave < 4:
                row = (wave % 2) * 32 + 2 * m + wave // 2
                sending[pl.ds(base, WITHIN), :] = child[pl.ds(row, WITHIN, stride=64), :]
            else:
                sending[pl.ds(base, WITHIN), :] = series[:, m * 128 : (m + 1) * 128]
    pl.semaphore_wait(barrier, 33)

    def slab(source, wave):
        return (source * WAVES + wave) * SLAB

    for wave in range(WAVES):
        own = slab(ring, wave) + plane * WITHIN

        def spread(i, carry):
            peer = plane_peer(i)
            pltpu.make_async_remote_copy(
                src_ref=sending.at[rows((wave * PLANE + peer) * WITHIN, WITHIN)],
                dst_ref=gathered.at[rows(own, WITHIN)],
                send_sem=a_send.at[wave],
                recv_sem=a_recv.at[wave],
                device_id=(half, z * 16 + peer, core),
                device_id_type=MESH,
            ).start()
            return carry

        lax.fori_loop(1, PLANE, spread, 0)
        pltpu.make_async_copy(
            sending.at[rows((wave * PLANE + plane) * WITHIN, WITHIN)], gathered.at[rows(own, WITHIN)], own_sem.at[wave]
        ).start()

    def spread_wait(wave):
        own = slab(ring, wave)
        count = (PLANE - 1) * WITHIN
        pltpu.make_async_remote_copy(
            src_ref=sending.at[pl.ds(wave * SLAB, count)],
            dst_ref=gathered.at[rows(own, count)],
            send_sem=a_send.at[wave],
            recv_sem=a_recv.at[wave],
            device_id=(half, point, 1 - core),
            device_id_type=MESH,
        ).wait()
        pltpu.make_async_copy(
            sending.at[pl.ds(0, WITHIN)], gathered.at[rows(own, WITHIN)], own_sem.at[wave]
        ).wait()

    def ring_copy(wave, direction, hop, part, source):
        place = rows(slab(source, wave) + part * PART, PART)
        target = ring_device((ring + (1 if direction == 0 else 7)) % 8)
        index = ((wave * 2 + direction) * HOPS + hop) * PARTS + part
        return pltpu.make_async_remote_copy(
            src_ref=gathered.at[place],
            dst_ref=gathered.at[place],
            send_sem=z_send.at[index],
            recv_sem=z_recv.at[index],
            device_id=target,
            device_id_type=MESH,
        )

    def origin(direction, hop):
        return (ring + (8 - hop if direction == 0 else hop)) % 8

    def begin(wave):
        for part in range(PARTS):
            for direction in range(2):

                @pl.when(reach(wave, ring, direction) >= 1)
                def _():
                    ring_copy(wave, direction, 0, part, ring).start()

    def relay(wave, hop):
        for part in range(PARTS):
            for direction in range(2):
                source = origin(direction, hop)
                extent = reach(wave, source, direction)

                @pl.when(extent >= hop)
                def _():
                    ring_copy(wave, direction, hop - 1, part, source).wait_recv()
                    if hop < HOPS:

                        @pl.when(extent >= hop + 1)
                        def _():
                            ring_copy(wave, direction, hop, part, source).start()

    def ring_finish():
        for wave in range(WAVES):
            for hop in range(HOPS):
                for direction in range(2):
                    source = origin(direction, hop)

                    @pl.when(reach(wave, source, direction) >= hop + 1)
                    def _():
                        for part in range(PARTS):
                            ring_copy(wave, direction, hop, part, source).wait_send()

    def transform(first, wave, slot, place):
        def over_t(step, carry):
            columns = []
            for k in range(2):
                t = step * 2 + k
                column = jnp.concatenate(
                    [gathered[pl.ds(slab(first + i, wave) + t, PLANE, stride=WITHIN), :] for i in range(4)], axis=0
                )
                columns.append(stacked_halves(column))
            out = dot(outer[...], jnp.concatenate(columns, axis=1))
            for k in range(2):
                t = step * 2 + k
                mid[rows(t * PLANE, PLANE), :] = out[:PLANE, k * 128 : (k + 1) * 128]
                mid[rows((WITHIN + t) * PLANE, PLANE), :] = out[PLANE:, k * 128 : (k + 1) * 128]
            return carry

        lax.fori_loop(0, WITHIN // 2, over_t, 0, unroll=2)

        def over_q(q, carry):
            values = mid[pl.ds(q, 2 * WITHIN, stride=PLANE), :]
            out = dot(inner[rows(q * 64, 64), :], stacked_halves(values))
            spectra[rows(slot * 1024 + q * 64, 64), :] = out
            return carry

        lax.fori_loop(0, PLANE, over_q, 0, unroll=2)

        def back(i, carry):
            peer = plane_peer(i)
            other = (core + i // 16) % 2
            pltpu.make_async_remote_copy(
                src_ref=spectra.at[rows(slot * 1024 + peer * 64 + other * 32, 32)],
                dst_ref=received.at[rows(place * 32, 32)],
                send_sem=d_send.at[slot],
                recv_sem=d_recv.at[slot],
                device_id=(half, z * 16 + peer, other),
                device_id_type=MESH,
            ).start()
            return carry

        lax.fori_loop(1, 32, back, 0)
        pltpu.make_async_copy(
            spectra.at[rows(slot * 1024 + plane * 64 + core * 32, 32)], received.at[rows(place * 32, 32)], own_sem.at[WAVES + slot]
        ).start()

    def back_wait(slot):
        pltpu.make_async_remote_copy(
            src_ref=spectra.at[pl.ds(slot * 1024, 31 * 32)],
            dst_ref=received.at[pl.ds(0, 31 * 32)],
            send_sem=d_send.at[slot],
            recv_sem=d_recv.at[slot],
            device_id=(half, point, 1 - core),
            device_id_type=MESH,
        ).wait()
        pltpu.make_async_copy(
            spectra.at[pl.ds(0, 32)], received.at[pl.ds(0, 32)], own_sem.at[WAVES + slot]
        ).wait()

    for tick in range(WAVES + HOPS):
        if tick == 0:
            spread_wait(0)
            begin(0)
        if tick + 1 < WAVES:
            spread_wait(tick + 1)
            begin(tick + 1)
        for wave in range(WAVES):
            hop = tick - wave
            if 1 <= hop <= HOPS and not (wave == 4 and hop == 5):
                relay(wave, hop)
        done = tick - HOPS
        if tick == HOPS:
            for copy in consts:
                copy.wait()
        if 0 <= done < 4:
            transform(0, done, done, core * 64 + (done % 2) * 32 + 2 * plane + done // 2)
            if done % 2 == 1:
                transform(4, done - 1 + half, 4 + done // 2, 128 + core * 32 + 2 * plane + done // 2)
        if done == 3:
            for side in range(2):
                transform(4 * side, 4, 6 + side, 192 + core * 32 + side * 16 + plane)

    ring_finish()
    for slot in range(6):
        back_wait(slot)

    def basis_point(s, carry):
        lower = [halves(received[pl.ds(c * 16 + s, 128, stride=32), :]) for c in range(2)]
        upper = [halves(received[pl.ds(128 * 32 + c * 16 + s, 64, stride=32), :]) for c in range(2)]
        right = [
            jnp.concatenate(
                [
                    jnp.concatenate([lower[0][k], lower[1][k]], axis=1),
                    jnp.concatenate([-lower[1][k], lower[0][k]], axis=1),
                ],
                axis=0,
            )
            for k in range(2)
        ]
        left = [jnp.concatenate([upper[0][k], upper[1][k]], axis=1) for k in range(2)]
        both = dot(jnp.concatenate(left, axis=0), right[0])
        out = both[:64] + both[64:] + dot(left[0], right[1])
        for r in range(2):
            for c in range(2):
                products[rows(((r * 2 + c) * 16 + s) * 32, 32), :] = out[r * 32 : (r + 1) * 32, c * 128 : (c + 1) * 128]
        return carry

    lax.fori_loop(0, 16, basis_point, 0)

    def basis_copies(c):
        place = rows(c * 1024 + core * 512, 512)
        return (
            pltpu.make_async_copy(products.at[rows((core * 2 + c) * 512, 512)], basis_out.at[place], out_local.at[c]),
            pltpu.make_async_remote_copy(
                src_ref=products.at[rows(((1 - core) * 2 + c) * 512, 512)],
                dst_ref=basis_out.at[place],
                send_sem=out_send.at[c],
                recv_sem=out_recv.at[c],
                device_id=(half, point, 1 - core),
                device_id_type=MESH,
            ),
        )

    def residual_copies(c):
        place = rows(c * 32 + core * 16, 16)
        return (
            pltpu.make_async_copy(lanes.at[rows((core * 2 + c) * 16, 16)], residual_out.at[place], out_local.at[2 + c]),
            pltpu.make_async_remote_copy(
                src_ref=lanes.at[rows(((1 - core) * 2 + c) * 16, 16)],
                dst_ref=residual_out.at[place],
                send_sem=out_send.at[2 + c],
                recv_sem=out_recv.at[2 + c],
                device_id=(half, point, 1 - core),
                device_id_type=MESH,
            ),
        )

    for c in range(2):
        for copy in basis_copies(c):
            copy.start()

    for slot in range(6, 8):
        back_wait(slot)
    first_lane = lax.broadcasted_iota(jnp.int32, (64, 128), 1) < 64
    first_lane_s = lax.broadcasted_iota(jnp.int32, (16, 128), 1) < 64

    def residual_point(s, carry):
        left = []
        for c in range(2):
            left.append(
                jnp.concatenate(
                    [received[pl.ds((r * 64 + 32 * half) * 32 + c * 16 + s, 32, stride=32), :] for r in range(2)], axis=0
                )
            )
        left = halves(jnp.concatenate(left, axis=1))
        real = received[pl.ds(192 * 32 + s, 64, stride=32), :]
        imag = received[pl.ds(192 * 32 + 16 + s, 64, stride=32), :]
        real_turn = pltpu.roll(real, 64, 1)
        imag_turn = pltpu.roll(imag, 64, 1)
        mixed[pl.ds(0, 64, stride=2), :] = jnp.where(first_lane, real, imag_turn)
        mixed[pl.ds(1, 64, stride=2), :] = jnp.where(first_lane, real_turn, imag)
        mixed[pl.ds(128, 64, stride=2), :] = jnp.where(first_lane, -imag, real_turn)
        mixed[pl.ds(129, 64, stride=2), :] = jnp.where(first_lane, -imag_turn, real)
        right = halves(mixed[...])
        both = dot(jnp.concatenate(left, axis=0), right[0])
        pairs[rows(s * 64, 64), :] = both[:64] + both[64:] + dot(left[0], right[1])
        return carry

    lax.fori_loop(0, 16, residual_point, 0)

    for r in range(2):
        for k in range(16):
            even = pairs[pl.ds(r * 32 + 2 * k, 16, stride=64), :]
            odd = pairs[pl.ds(r * 32 + 2 * k + 1, 16, stride=64), :]
            lanes[pl.ds((r * 2) * 16, 16), k * 128 : (k + 1) * 128] = jnp.where(first_lane_s, even, pltpu.roll(odd, 64, 1))
            lanes[pl.ds((r * 2 + 1) * 16, 16), k * 128 : (k + 1) * 128] = jnp.where(first_lane_s, pltpu.roll(even, 64, 1), odd)

    for c in range(2):
        for copy in residual_copies(c):
            copy.start()
    for c in range(2):
        for copy in basis_copies(c) + residual_copies(c):
            copy.wait()


def per_device(children, residual_series):
    outer, inner = transform_matrices()
    vmem = pl.BlockSpec(memory_space=pltpu.VMEM)
    anywhere = pl.BlockSpec(memory_space=pl.ANY)
    basis, residual = pl.pallas_call(
        kernel,
        name="merge",
        out_shape=(
            jax.ShapeDtypeStruct((2 * WITHIN * 32, 128), F32),
            jax.ShapeDtypeStruct((2 * WITHIN, 2048), F32),
        ),
        in_specs=[vmem, vmem, anywhere, anywhere],
        out_specs=(anywhere, anywhere),
        scratch_shapes=[
            pltpu.VMEM((RING * WAVES * SLAB, 128), F32),
            pltpu.VMEM((WAVES * SLAB, 128), F32),
            pltpu.VMEM((2 * WITHIN * PLANE, 128), F32),
            pltpu.VMEM((8 * 1024, 128), F32),
            pltpu.VMEM((256 * 32, 128), F32),
            pltpu.VMEM((4 * 512, 128), F32),
            pltpu.VMEM((16 * 64, 128), F32),
            pltpu.VMEM((256, 128), F32),
            pltpu.VMEM((64, 2048), F32),
            pltpu.VMEM((32, 256), BF16),
            pltpu.VMEM((PLANE * 64, 256), BF16),
            pltpu.SemaphoreType.DMA((WAVES,)),
            pltpu.SemaphoreType.DMA((WAVES,)),
            pltpu.SemaphoreType.DMA((WAVES + 8,)),
            pltpu.SemaphoreType.DMA((WAVES * 2 * HOPS * PARTS,)),
            pltpu.SemaphoreType.DMA((WAVES * 2 * HOPS * PARTS,)),
            pltpu.SemaphoreType.DMA((8,)),
            pltpu.SemaphoreType.DMA((8,)),
            pltpu.SemaphoreType.DMA((2,)),
            pltpu.SemaphoreType.DMA((4,)),
            pltpu.SemaphoreType.DMA((4,)),
            pltpu.SemaphoreType.DMA((4,)),
        ],
        compiler_params=pltpu.CompilerParams(collective_id=0, has_side_effects=True, vmem_limit_bytes=48 * 2**20),
    )(
        children.reshape(WITHIN * 64, 128),
        residual_series,
        jnp.asarray(outer),
        jnp.asarray(inner),
    )
    return basis.reshape(2, WITHIN, 32, 128), residual.reshape(2, WITHIN, 2048)


def solution(mesh):
    placed = (P("half", "point", "row", None), P("point", ("row", "half")))
    return jax.shard_map(
        per_device,
        mesh=mesh,
        in_specs=placed,
        out_specs=(P(None, "point", ("row", "half"), None), P(None, "point", ("row", "half"))),
        check_vma=False,
    )
```

```python
import math

import jax
import jax.numpy as jnp
import numpy as np
from jax import lax
from jax.experimental import pallas as pl
from jax.experimental.pallas import tpu as pltpu
from jax.sharding import PartitionSpec as P

BASIS = 128
BLOCK = 64
LENGTH = 524288
WITHIN = 32
GROUPS = 64
PLANE = 16
RING = 8
WAVES = 5
HOPS = 5
PARTS = 4
SLAB = PLANE * WITHIN
PART = SLAB // PARTS
STARTS = {"L0": 1, "L1": 2, "L2": 3, "L3": 5, "U0": 1, "U1": 4, "S0": 8, "S1": 8}
LEAD = 1
MESH = pl.DeviceIdType.MESH
F32 = jnp.float32
BF16 = jnp.bfloat16


def split_matrix(matrix):
    matrix = matrix.astype(np.float32)
    high = matrix.astype(jnp.bfloat16)
    low = (matrix - high.astype(np.float32)).astype(jnp.bfloat16)
    return np.concatenate([high, high, low, low], axis=-1)


def transform_matrices():
    q = np.arange(GROUPS).reshape(4, PLANE)
    p = np.arange(GROUPS)
    phase = (32 * p[None, None, :] * (256 * q[:, :, None] + 1)) % LENGTH
    angle = phase * (2.0 * math.pi / LENGTH)
    outer = np.concatenate([np.cos(angle), np.sin(angle)], axis=1)
    t = np.arange(WITHIN)
    s = np.arange(WITHIN)
    phase = t[None, None, None, :] * (s[None, None, :, None] * 16384 + 256 * q[:, :, None, None] + 1)
    angle = (phase % LENGTH) * (2.0 * math.pi / LENGTH)
    cos, sin = np.cos(angle), np.sin(angle)
    real = np.concatenate([cos, -sin], axis=-1).reshape(4, PLANE, 2, 1, 16, 64)
    imag = np.concatenate([sin, cos], axis=-1).reshape(4, PLANE, 2, 1, 16, 64)
    inner = np.concatenate([real, imag], axis=3).reshape(4, PLANE * 64, 64)
    return split_matrix(outer), split_matrix(inner)


def halves(x):
    high = x.astype(BF16)
    return high, (x - high.astype(F32)).astype(BF16)


def stacked_halves(x):
    high, low = halves(x)
    return jnp.concatenate([high, low, high, low], axis=0)


def dot(a, b):
    return jnp.dot(a, b, preferred_element_type=F32)


def rows(offset, count):
    return pl.ds(pl.multiple_of(offset, 8), count)


def parts_of(item):
    return range(2 * PARTS if item[0] == "U" else PARTS)


def waves_of(item):
    kind, number = item[0], int(item[1])
    return {"L": [number], "U": [2 * number, 2 * number + 1], "S": [4]}[kind]


def reach(item, source, direction, part):
    in_lower = source < 4
    if item[0] == "L":
        return jnp.where(in_lower, source + 2 if direction == 0 else 5 - source, 0)
    if item[0] == "S":
        hops = 4 if (direction == 0) == (part < PARTS // 2) else 3
        return jnp.where(in_lower if item == "S0" else source >= 4, hops, 0)
    if part % 2 == 1:
        hops = 7 - source if direction == 0 else source - 4
    elif direction == 0:
        hops = jnp.where(source >= 6, 11 - source, 0)
    else:
        hops = jnp.where(source <= 5, source, 0)
    return jnp.where(in_lower, 0, hops)


def longest(item, direction, part):
    if item[0] == "S":
        return 4 if (direction == 0) == (part < PARTS // 2) else 3
    if item[0] == "U" and part % 2 == 1:
        return 3
    return 5


def kernel(
    child_in, series_in, outer_all, inner_all, basis_out, residual_out,
    child, series, gathered, sending, mid, spectra, received, products, pairs, mixed, lanes, outer, inner,
    a_send, a_recv, own_sem, z_send, z_recv, d_send, d_recv, const_sem, out_local, out_send, out_recv,
):
    half = lax.axis_index("half")
    point = lax.axis_index("point")
    core = lax.axis_index("row")
    z = point // 16
    plane = point % 16
    y = plane // 4
    x = plane % 4
    ring = half * 4 + z

    def plane_peer(i):
        dy, dx = (i // 4) % 4, i % 4
        return ((y + dy) % 4) * 4 + (x + dx) % 4

    def ring_device(position):
        return (position // 4, (position % 4) * 16 + plane, core)

    consts = [
        pltpu.make_async_copy(outer_all.at[z], outer, const_sem.at[0]),
        pltpu.make_async_copy(inner_all.at[z], inner, const_sem.at[1]),
    ]
    loads = [
        pltpu.make_async_copy(child_in, child, const_sem.at[2]),
        pltpu.make_async_copy(series_in, series, const_sem.at[3]),
    ]
    for copy in loads + consts:
        copy.start()

    barrier = pltpu.get_barrier_semaphore()

    def greet(i, carry):
        peer = plane_peer(i)
        pl.semaphore_signal(barrier, inc=1, device_id=(half, z * 16 + peer, (core + i // 16) % 2), device_id_type=MESH)
        return carry

    lax.fori_loop(1, 32, greet, 0)
    for step in (1, 7):
        pl.semaphore_signal(barrier, inc=1, device_id=ring_device((ring + step) % 8), device_id_type=MESH)

    for wave in range(WAVES):
        if wave in (0, 4):
            loads[wave // 4].wait()
        for m in range(PLANE):
            base = (wave * PLANE + m) * WITHIN
            if wave < 4:
                row = (wave % 2) * 32 + 2 * m + wave // 2
                sending[pl.ds(base, WITHIN), :] = child[pl.ds(row, WITHIN, stride=64), :]
            else:
                sending[pl.ds(base, WITHIN), :] = series[:, m * 128 : (m + 1) * 128]
    pl.semaphore_wait(barrier, 33)

    def slab(source, wave):
        return (source * WAVES + wave) * SLAB

    def spread(wave):
        own = slab(ring, wave) + plane * WITHIN

        def send(i, carry):
            peer = plane_peer(i)
            pltpu.make_async_remote_copy(
                src_ref=sending.at[rows((wave * PLANE + peer) * WITHIN, WITHIN)],
                dst_ref=gathered.at[rows(own, WITHIN)],
                send_sem=a_send.at[wave],
                recv_sem=a_recv.at[wave],
                device_id=(half, z * 16 + peer, core),
                device_id_type=MESH,
            ).start()
            return carry

        lax.fori_loop(1, PLANE, send, 0)
        pltpu.make_async_copy(
            sending.at[rows((wave * PLANE + plane) * WITHIN, WITHIN)], gathered.at[rows(own, WITHIN)], own_sem.at[wave]
        ).start()

    def spread_wait(wave):
        own = slab(ring, wave)
        count = (PLANE - 1) * WITHIN
        pltpu.make_async_remote_copy(
            src_ref=sending.at[pl.ds(wave * SLAB, count)],
            dst_ref=gathered.at[rows(own, count)],
            send_sem=a_send.at[wave],
            recv_sem=a_recv.at[wave],
            device_id=(half, point, 1 - core),
            device_id_type=MESH,
        ).wait()
        pltpu.make_async_copy(
            sending.at[pl.ds(0, WITHIN)], gathered.at[rows(own, WITHIN)], own_sem.at[wave]
        ).wait()

    def ring_copy(item, direction, hop, part, source):
        number = int(item[1])
        if item[0] == "U":
            offset = slab(source, 2 * number + part % 2) + part // 2 * PART
            stream = 2 * number * PARTS + part
        else:
            wave = waves_of(item)[0]
            offset = slab(source, wave) + part * PART
            stream = wave * PARTS + part
        place = rows(offset, PART)
        index = (stream * 2 + direction) * HOPS + hop
        return pltpu.make_async_remote_copy(
            src_ref=gathered.at[place],
            dst_ref=gathered.at[place],
            send_sem=z_send.at[index],
            recv_sem=z_recv.at[index],
            device_id=ring_device((ring + (1 if direction == 0 else 7)) % 8),
            device_id_type=MESH,
        )

    def origin(direction, hop):
        return (ring + (8 - hop if direction == 0 else hop)) % 8

    def begin(item):
        for part in parts_of(item):
            for direction in range(2):

                @pl.when(reach(item, ring, direction, part) >= 1)
                def _():
                    ring_copy(item, direction, 0, part, ring).start()

    def relay(item, hop):
        for part in parts_of(item):
            for direction in range(2):
                if longest(item, direction, part) < hop:
                    continue
                source = origin(direction, hop)
                extent = reach(item, source, direction, part)

                @pl.when(extent >= hop)
                def _():
                    ring_copy(item, direction, hop - 1, part, source).wait_recv()
                    if longest(item, direction, part) > hop:

                        @pl.when(extent > hop)
                        def _():
                            ring_copy(item, direction, hop, part, source).start()

    def ring_finish():
        for item in STARTS:
            for part in parts_of(item):
                for direction in range(2):
                    for hop in range(longest(item, direction, part)):
                        source = origin(direction, hop)

                        @pl.when(reach(item, source, direction, part) > hop)
                        def _():
                            ring_copy(item, direction, hop, part, source).wait_send()

    def transform(first, wave, slot, place):
        def over_t(step, carry):
            columns = []
            for k in range(2):
                t = step * 2 + k
                column = jnp.concatenate(
                    [gathered[pl.ds(slab(first + i, wave) + t, PLANE, stride=WITHIN), :] for i in range(4)], axis=0
                )
                columns.append(stacked_halves(column))
            out = dot(outer[...], jnp.concatenate(columns, axis=1))
            for k in range(2):
                t = step * 2 + k
                mid[rows(t * PLANE, PLANE), :] = out[:PLANE, k * 128 : (k + 1) * 128]
                mid[rows((WITHIN + t) * PLANE, PLANE), :] = out[PLANE:, k * 128 : (k + 1) * 128]
            return carry

        lax.fori_loop(0, WITHIN // 2, over_t, 0, unroll=2)

        def over_q(q, carry):
            values = mid[pl.ds(q, 2 * WITHIN, stride=PLANE), :]
            out = dot(inner[rows(q * 64, 64), :], stacked_halves(values))
            spectra[rows(slot * 1024 + q * 64, 64), :] = out
            return carry

        lax.fori_loop(0, PLANE, over_q, 0, unroll=2)

        def back(i, carry):
            peer = plane_peer(i)
            other = (core + i // 16) % 2
            pltpu.make_async_remote_copy(
                src_ref=spectra.at[rows(slot * 1024 + peer * 64 + other * 32, 32)],
                dst_ref=received.at[rows(place * 32, 32)],
                send_sem=d_send.at[slot],
                recv_sem=d_recv.at[slot],
                device_id=(half, z * 16 + peer, other),
                device_id_type=MESH,
            ).start()
            return carry

        lax.fori_loop(1, 32, back, 0)
        pltpu.make_async_copy(
            spectra.at[rows(slot * 1024 + plane * 64 + core * 32, 32)], received.at[rows(place * 32, 32)], own_sem.at[WAVES + slot]
        ).start()

    def back_wait(slot):
        pltpu.make_async_remote_copy(
            src_ref=spectra.at[pl.ds(slot * 1024, 31 * 32)],
            dst_ref=received.at[pl.ds(0, 31 * 32)],
            send_sem=d_send.at[slot],
            recv_sem=d_recv.at[slot],
            device_id=(half, point, 1 - core),
            device_id_type=MESH,
        ).wait()
        pltpu.make_async_copy(
            spectra.at[pl.ds(0, 32)], received.at[pl.ds(0, 32)], own_sem.at[WAVES + slot]
        ).wait()

    for wave in range(WAVES):
        spread(wave)

    events = []
    for item, start in STARTS.items():
        last = 4 if item[0] == "S" else HOPS
        events.append((start - LEAD, 1, start, item, 0))
        events += [(start + hop, 0, start, item, hop) for hop in range(1, last + 1)]
        events.append((start + last, 2, start, item, 0))
    ready = set()
    ready_consts = False
    for _, kind, _, item, hop in sorted(events):
        number = int(item[1])
        if kind == 0:
            relay(item, hop)
        elif kind == 1:
            for wave in waves_of(item):
                if wave not in ready:
                    spread_wait(wave)
                    ready.add(wave)
            begin(item)
        else:
            if not ready_consts:
                for copy in consts:
                    copy.wait()
                ready_consts = True
            if item[0] == "L":
                transform(0, number, number, core * 64 + number % 2 * 32 + 2 * plane + number // 2)
            elif item[0] == "U":
                transform(4, 2 * number + half, 4 + number, 128 + core * 32 + 2 * plane + number)
            else:
                transform(4 * number, 4, 6 + number, 192 + core * 32 + number * 16 + plane)

    ring_finish()
    for slot in range(6):
        back_wait(slot)

    def basis_point(s, carry):
        lower = [halves(received[pl.ds(c * 16 + s, 128, stride=32), :]) for c in range(2)]
        upper = [halves(received[pl.ds(128 * 32 + c * 16 + s, 64, stride=32), :]) for c in range(2)]
        right = [
            jnp.concatenate(
                [
                    jnp.concatenate([lower[0][k], lower[1][k]], axis=1),
                    jnp.concatenate([-lower[1][k], lower[0][k]], axis=1),
                ],
                axis=0,
            )
            for k in range(2)
        ]
        left = [jnp.concatenate([upper[0][k], upper[1][k]], axis=1) for k in range(2)]
        both = dot(jnp.concatenate(left, axis=0), right[0])
        out = both[:64] + both[64:] + dot(left[0], right[1])
        for r in range(2):
            for c in range(2):
                products[rows(((r * 2 + c) * 16 + s) * 32, 32), :] = out[r * 32 : (r + 1) * 32, c * 128 : (c + 1) * 128]
        return carry

    lax.fori_loop(0, 16, basis_point, 0)

    def basis_copies(c):
        place = rows(c * 1024 + core * 512, 512)
        return (
            pltpu.make_async_copy(products.at[rows((core * 2 + c) * 512, 512)], basis_out.at[place], out_local.at[c]),
            pltpu.make_async_remote_copy(
                src_ref=products.at[rows(((1 - core) * 2 + c) * 512, 512)],
                dst_ref=basis_out.at[place],
                send_sem=out_send.at[c],
                recv_sem=out_recv.at[c],
                device_id=(half, point, 1 - core),
                device_id_type=MESH,
            ),
        )

    def residual_copies(c):
        place = rows(c * 32 + core * 16, 16)
        return (
            pltpu.make_async_copy(lanes.at[rows((core * 2 + c) * 16, 16)], residual_out.at[place], out_local.at[2 + c]),
            pltpu.make_async_remote_copy(
                src_ref=lanes.at[rows(((1 - core) * 2 + c) * 16, 16)],
                dst_ref=residual_out.at[place],
                send_sem=out_send.at[2 + c],
                recv_sem=out_recv.at[2 + c],
                device_id=(half, point, 1 - core),
                device_id_type=MESH,
            ),
        )

    for c in range(2):
        for copy in basis_copies(c):
            copy.start()

    for slot in range(6, 8):
        back_wait(slot)
    first_lane = lax.broadcasted_iota(jnp.int32, (64, 128), 1) < 64
    first_lane_s = lax.broadcasted_iota(jnp.int32, (16, 128), 1) < 64

    def residual_point(s, carry):
        left = []
        for c in range(2):
            left.append(
                jnp.concatenate(
                    [received[pl.ds((r * 64 + 32 * half) * 32 + c * 16 + s, 32, stride=32), :] for r in range(2)], axis=0
                )
            )
        left = halves(jnp.concatenate(left, axis=1))
        real = received[pl.ds(192 * 32 + s, 64, stride=32), :]
        imag = received[pl.ds(192 * 32 + 16 + s, 64, stride=32), :]
        real_turn = pltpu.roll(real, 64, 1)
        imag_turn = pltpu.roll(imag, 64, 1)
        mixed[pl.ds(0, 64, stride=2), :] = jnp.where(first_lane, real, imag_turn)
        mixed[pl.ds(1, 64, stride=2), :] = jnp.where(first_lane, real_turn, imag)
        mixed[pl.ds(128, 64, stride=2), :] = jnp.where(first_lane, -imag, real_turn)
        mixed[pl.ds(129, 64, stride=2), :] = jnp.where(first_lane, -imag_turn, real)
        right = halves(mixed[...])
        both = dot(jnp.concatenate(left, axis=0), right[0])
        pairs[rows(s * 64, 64), :] = both[:64] + both[64:] + dot(left[0], right[1])
        return carry

    lax.fori_loop(0, 16, residual_point, 0)

    for r in range(2):
        for k in range(16):
            even = pairs[pl.ds(r * 32 + 2 * k, 16, stride=64), :]
            odd = pairs[pl.ds(r * 32 + 2 * k + 1, 16, stride=64), :]
            lanes[pl.ds((r * 2) * 16, 16), k * 128 : (k + 1) * 128] = jnp.where(first_lane_s, even, pltpu.roll(odd, 64, 1))
            lanes[pl.ds((r * 2 + 1) * 16, 16), k * 128 : (k + 1) * 128] = jnp.where(first_lane_s, pltpu.roll(even, 64, 1), odd)

    for c in range(2):
        for copy in residual_copies(c):
            copy.start()
    for c in range(2):
        for copy in basis_copies(c) + residual_copies(c):
            copy.wait()


def per_device(children, residual_series):
    outer, inner = transform_matrices()
    hbm = pl.BlockSpec(memory_space=pltpu.HBM)
    basis, residual = pl.pallas_call(
        kernel,
        name="merge",
        out_shape=(
            jax.ShapeDtypeStruct((2 * WITHIN * 32, 128), F32),
            jax.ShapeDtypeStruct((2 * WITHIN, 2048), F32),
        ),
        in_specs=[hbm] * 4,
        out_specs=(hbm, hbm),
        scratch_shapes=[
            pltpu.VMEM((WITHIN * 64, 128), F32),
            pltpu.VMEM((WITHIN, 2048), F32),
            pltpu.VMEM((RING * WAVES * SLAB, 128), F32),
            pltpu.VMEM((WAVES * SLAB, 128), F32),
            pltpu.VMEM((2 * WITHIN * PLANE, 128), F32),
            pltpu.VMEM((8 * 1024, 128), F32),
            pltpu.VMEM((256 * 32, 128), F32),
            pltpu.VMEM((4 * 512, 128), F32),
            pltpu.VMEM((16 * 64, 128), F32),
            pltpu.VMEM((256, 128), F32),
            pltpu.VMEM((64, 2048), F32),
            pltpu.VMEM((32, 256), BF16),
            pltpu.VMEM((PLANE * 64, 256), BF16),
            pltpu.SemaphoreType.DMA((WAVES,)),
            pltpu.SemaphoreType.DMA((WAVES,)),
            pltpu.SemaphoreType.DMA((WAVES + 8,)),
            pltpu.SemaphoreType.DMA((WAVES * PARTS * 2 * HOPS,)),
            pltpu.SemaphoreType.DMA((WAVES * PARTS * 2 * HOPS,)),
            pltpu.SemaphoreType.DMA((8,)),
            pltpu.SemaphoreType.DMA((8,)),
            pltpu.SemaphoreType.DMA((4,)),
            pltpu.SemaphoreType.DMA((4,)),
            pltpu.SemaphoreType.DMA((4,)),
            pltpu.SemaphoreType.DMA((4,)),
        ],
        compiler_params=pltpu.CompilerParams(collective_id=0, has_side_effects=True, vmem_limit_bytes=62 * 2**20),
    )(
        children.reshape(WITHIN * 64, 128),
        residual_series,
        jnp.asarray(outer),
        jnp.asarray(inner),
    )
    return basis.reshape(2, WITHIN, 32, 128), residual.reshape(2, WITHIN, 2048)


def solution(mesh):
    placed = (P("half", "point", "row", None), P("point", ("row", "half")))
    return jax.shard_map(
        per_device,
        mesh=mesh,
        in_specs=placed,
        out_specs=(P(None, "point", ("row", "half"), None), P(None, "point", ("row", "half"))),
        check_vma=False,
    )
```

```python
import math

import jax
import jax.numpy as jnp
import numpy as np
from jax import lax
from jax.experimental import pallas as pl
from jax.experimental.pallas import tpu as pltpu
from jax.sharding import PartitionSpec as P

BASIS = 128
BLOCK = 64
LENGTH = 524288
WITHIN = 32
GROUPS = 64
PLANE = 16
RING = 8
WAVES = 5
HOPS = 5
PARTS = 4
SLAB = PLANE * WITHIN
PART = SLAB // PARTS
STARTS = {"L0": 1, "L1": 2, "L2": 3, "L3": 5, "U0": 1, "U1": 4, "S0": 8, "S1": 8}
LEAD = 1
MESH = pl.DeviceIdType.MESH
F32 = jnp.float32
BF16 = jnp.bfloat16


def split_matrix(matrix):
    matrix = matrix.astype(np.float32)
    high = matrix.astype(jnp.bfloat16)
    low = (matrix - high.astype(np.float32)).astype(jnp.bfloat16)
    return np.concatenate([high, high, low, low], axis=-1)


def transform_matrices():
    q = np.arange(GROUPS).reshape(4, PLANE)
    p = np.arange(GROUPS)
    phase = (32 * p[None, None, :] * (256 * q[:, :, None] + 1)) % LENGTH
    angle = phase * (2.0 * math.pi / LENGTH)
    outer = np.concatenate([np.cos(angle), np.sin(angle)], axis=1)
    t = np.arange(WITHIN)
    s = np.arange(WITHIN)
    phase = t[None, None, None, :] * (s[None, None, :, None] * 16384 + 256 * q[:, :, None, None] + 1)
    angle = (phase % LENGTH) * (2.0 * math.pi / LENGTH)
    cos, sin = np.cos(angle), np.sin(angle)
    real = np.concatenate([cos, -sin], axis=-1).reshape(4, PLANE, 2, 1, 16, 64)
    imag = np.concatenate([sin, cos], axis=-1).reshape(4, PLANE, 2, 1, 16, 64)
    inner = np.concatenate([real, imag], axis=3).reshape(4, PLANE * 64, 64)
    return split_matrix(outer), split_matrix(inner)


def halves(x):
    high = x.astype(BF16)
    return high, (x - high.astype(F32)).astype(BF16)


def stacked_halves(x):
    high, low = halves(x)
    return jnp.concatenate([high, low, high, low], axis=0)


def dot(a, b):
    return jnp.dot(a, b, preferred_element_type=F32)


def rows(offset, count):
    return pl.ds(pl.multiple_of(offset, 8), count)


def parts_of(item):
    return range(2 * PARTS if item[0] == "U" else PARTS)


def waves_of(item):
    kind, number = item[0], int(item[1])
    return {"L": [number], "U": [2 * number, 2 * number + 1], "S": [4]}[kind]


def reach(item, source, direction, part):
    in_lower = source < 4
    if item[0] == "L":
        return jnp.where(in_lower, source + 2 if direction == 0 else 5 - source, 0)
    if item[0] == "S":
        hops = 4 if (direction == 0) == (part < PARTS // 2) else 3
        return jnp.where(in_lower if item == "S0" else source >= 4, hops, 0)
    if part % 2 == 1:
        hops = 7 - source if direction == 0 else source - 4
    elif direction == 0:
        hops = jnp.where(source >= 6, 11 - source, 0)
    else:
        hops = jnp.where(source <= 5, source, 0)
    return jnp.where(in_lower, 0, hops)


def longest(item, direction, part):
    if item[0] == "S":
        return 4 if (direction == 0) == (part < PARTS // 2) else 3
    if item[0] == "U" and part % 2 == 1:
        return 3
    return 5


def kernel(
    child_in, series_in, outer_all, inner_all, basis_out, residual_out,
    child, series, gathered, sending, mid, spectra, received, products, pairs, mixed, lanes, outer, inner,
    a_send, a_recv, own_sem, z_send, z_recv, d_send, d_recv, const_sem, out_local, out_send, out_recv,
):
    half = lax.axis_index("half")
    point = lax.axis_index("point")
    core = lax.axis_index("row")
    z = point // 16
    plane = point % 16
    y = plane // 4
    x = plane % 4
    ring = half * 4 + z

    def plane_peer(i):
        dy, dx = (i // 4) % 4, i % 4
        return ((y + dy) % 4) * 4 + (x + dx) % 4

    def ring_device(position):
        return (position // 4, (position % 4) * 16 + plane, core)

    consts = [
        pltpu.make_async_copy(outer_all.at[z], outer, const_sem.at[0]),
        pltpu.make_async_copy(inner_all.at[z], inner, const_sem.at[1]),
    ]
    loads = [
        pltpu.make_async_copy(child_in, child, const_sem.at[2]),
        pltpu.make_async_copy(series_in, series, const_sem.at[3]),
    ]
    for copy in loads + consts:
        copy.start()

    barrier = pltpu.get_barrier_semaphore()

    def greet(i, carry):
        peer = plane_peer(i)
        pl.semaphore_signal(barrier, inc=1, device_id=(half, z * 16 + peer, (core + i // 16) % 2), device_id_type=MESH)
        return carry

    lax.fori_loop(1, 32, greet, 0)
    for step in (1, 7):
        pl.semaphore_signal(barrier, inc=1, device_id=ring_device((ring + step) % 8), device_id_type=MESH)

    for wave in range(WAVES):
        if wave in (0, 4):
            loads[wave // 4].wait()
        for m in range(PLANE):
            base = (wave * PLANE + m) * WITHIN
            if wave < 4:
                row = (wave % 2) * 32 + 2 * m + wave // 2
                sending[pl.ds(base, WITHIN), :] = child[pl.ds(row, WITHIN, stride=64), :]
            else:
                sending[pl.ds(base, WITHIN), :] = series[:, m * 128 : (m + 1) * 128]
    pl.semaphore_wait(barrier, 33)

    def slab(source, wave):
        return (source * WAVES + wave) * SLAB

    def spread(wave):
        own = slab(ring, wave) + plane * WITHIN

        def send(i, carry):
            peer = plane_peer(i)
            pltpu.make_async_remote_copy(
                src_ref=sending.at[rows((wave * PLANE + peer) * WITHIN, WITHIN)],
                dst_ref=gathered.at[rows(own, WITHIN)],
                send_sem=a_send.at[wave],
                recv_sem=a_recv.at[wave],
                device_id=(half, z * 16 + peer, core),
                device_id_type=MESH,
            ).start()
            return carry

        lax.fori_loop(1, PLANE, send, 0)
        pltpu.make_async_copy(
            sending.at[rows((wave * PLANE + plane) * WITHIN, WITHIN)], gathered.at[rows(own, WITHIN)], own_sem.at[wave]
        ).start()

    def spread_wait(wave):
        own = slab(ring, wave)
        count = (PLANE - 1) * WITHIN
        pltpu.make_async_remote_copy(
            src_ref=sending.at[pl.ds(wave * SLAB, count)],
            dst_ref=gathered.at[rows(own, count)],
            send_sem=a_send.at[wave],
            recv_sem=a_recv.at[wave],
            device_id=(half, point, 1 - core),
            device_id_type=MESH,
        ).wait()
        pltpu.make_async_copy(
            sending.at[pl.ds(0, WITHIN)], gathered.at[rows(own, WITHIN)], own_sem.at[wave]
        ).wait()

    def ring_copy(item, direction, hop, part, source):
        number = int(item[1])
        if item[0] == "U":
            offset = slab(source, 2 * number + part % 2) + part // 2 * PART
            stream = 2 * number * PARTS + part
        else:
            wave = waves_of(item)[0]
            offset = slab(source, wave) + part * PART
            stream = wave * PARTS + part
        place = rows(offset, PART)
        index = (stream * 2 + direction) * HOPS + hop
        return pltpu.make_async_remote_copy(
            src_ref=gathered.at[place],
            dst_ref=gathered.at[place],
            send_sem=z_send.at[index],
            recv_sem=z_recv.at[index],
            device_id=ring_device((ring + (1 if direction == 0 else 7)) % 8),
            device_id_type=MESH,
        )

    def origin(direction, hop):
        return (ring + (8 - hop if direction == 0 else hop)) % 8

    def begin(item):
        for part in parts_of(item):
            for direction in range(2):

                @pl.when(reach(item, ring, direction, part) >= 1)
                def _():
                    ring_copy(item, direction, 0, part, ring).start()

    def relay(item, hop):
        for part in parts_of(item):
            for direction in range(2):
                if longest(item, direction, part) < hop:
                    continue
                source = origin(direction, hop)
                extent = reach(item, source, direction, part)

                @pl.when(extent >= hop)
                def _():
                    ring_copy(item, direction, hop - 1, part, source).wait_recv()
                    if longest(item, direction, part) > hop:

                        @pl.when(extent > hop)
                        def _():
                            ring_copy(item, direction, hop, part, source).start()

    def ring_finish():
        for item in STARTS:
            for part in parts_of(item):
                for direction in range(2):
                    for hop in range(longest(item, direction, part)):
                        source = origin(direction, hop)

                        @pl.when(reach(item, source, direction, part) > hop)
                        def _():
                            ring_copy(item, direction, hop, part, source).wait_send()

    def transform(first, wave, slot, place):
        def over_t(step, carry):
            columns = []
            for k in range(2):
                t = step * 2 + k
                column = jnp.concatenate(
                    [gathered[pl.ds(slab(first + i, wave) + t, PLANE, stride=WITHIN), :] for i in range(4)], axis=0
                )
                columns.append(stacked_halves(column))
            out = dot(outer[...], jnp.concatenate(columns, axis=1))
            for k in range(2):
                t = step * 2 + k
                mid[rows(t * PLANE, PLANE), :] = out[:PLANE, k * 128 : (k + 1) * 128]
                mid[rows((WITHIN + t) * PLANE, PLANE), :] = out[PLANE:, k * 128 : (k + 1) * 128]
            return carry

        lax.fori_loop(0, WITHIN // 2, over_t, 0, unroll=16)

        def over_q(q, carry):
            values = mid[pl.ds(q, 2 * WITHIN, stride=PLANE), :]
            out = dot(inner[rows(q * 64, 64), :], stacked_halves(values))
            spectra[rows(slot * 1024 + q * 64, 64), :] = out
            return carry

        lax.fori_loop(0, PLANE, over_q, 0, unroll=16)

        def back(i, carry):
            peer = plane_peer(i)
            other = (core + i // 16) % 2
            pltpu.make_async_remote_copy(
                src_ref=spectra.at[rows(slot * 1024 + peer * 64 + other * 32, 32)],
                dst_ref=received.at[rows(place * 32, 32)],
                send_sem=d_send.at[slot],
                recv_sem=d_recv.at[slot],
                device_id=(half, z * 16 + peer, other),
                device_id_type=MESH,
            ).start()
            return carry

        lax.fori_loop(1, 32, back, 0, unroll=4)
        pltpu.make_async_copy(
            spectra.at[rows(slot * 1024 + plane * 64 + core * 32, 32)], received.at[rows(place * 32, 32)], own_sem.at[WAVES + slot]
        ).start()

    def back_wait(slot):
        pltpu.make_async_remote_copy(
            src_ref=spectra.at[pl.ds(slot * 1024, 31 * 32)],
            dst_ref=received.at[pl.ds(0, 31 * 32)],
            send_sem=d_send.at[slot],
            recv_sem=d_recv.at[slot],
            device_id=(half, point, 1 - core),
            device_id_type=MESH,
        ).wait()
        pltpu.make_async_copy(
            spectra.at[pl.ds(0, 32)], received.at[pl.ds(0, 32)], own_sem.at[WAVES + slot]
        ).wait()

    for wave in range(WAVES):
        spread(wave)

    events = []
    for item, start in STARTS.items():
        last = 4 if item[0] == "S" else HOPS
        events.append((start - LEAD, 1, start, item, 0))
        events += [(start + hop, 0, start, item, hop) for hop in range(1, last + 1)]
        events.append((start + last, 2, start, item, 0))
    ready = set()
    ready_consts = False
    for _, kind, _, item, hop in sorted(events):
        number = int(item[1])
        if kind == 0:
            relay(item, hop)
        elif kind == 1:
            for wave in waves_of(item):
                if wave not in ready:
                    spread_wait(wave)
                    ready.add(wave)
            begin(item)
        else:
            if not ready_consts:
                for copy in consts:
                    copy.wait()
                ready_consts = True
            if item[0] == "L":
                transform(0, number, number, core * 64 + number % 2 * 32 + 2 * plane + number // 2)
            elif item[0] == "U":
                transform(4, 2 * number + half, 4 + number, 128 + core * 32 + 2 * plane + number)
            else:
                transform(4 * number, 4, 6 + number, 192 + core * 32 + number * 16 + plane)

    ring_finish()
    for slot in range(6):
        back_wait(slot)

    def basis_point(s, carry):
        lower = [halves(received[pl.ds(c * 16 + s, 128, stride=32), :]) for c in range(2)]
        upper = [halves(received[pl.ds(128 * 32 + c * 16 + s, 64, stride=32), :]) for c in range(2)]
        right = [
            jnp.concatenate(
                [
                    jnp.concatenate([lower[0][k], lower[1][k]], axis=1),
                    jnp.concatenate([-lower[1][k], lower[0][k]], axis=1),
                ],
                axis=0,
            )
            for k in range(2)
        ]
        left = [jnp.concatenate([upper[0][k], upper[1][k]], axis=1) for k in range(2)]
        both = dot(jnp.concatenate(left, axis=0), right[0])
        out = both[:64] + both[64:] + dot(left[0], right[1])
        for r in range(2):
            for c in range(2):
                products[rows(((r * 2 + c) * 16 + s) * 32, 32), :] = out[r * 32 : (r + 1) * 32, c * 128 : (c + 1) * 128]
        return carry

    lax.fori_loop(0, 16, basis_point, 0, unroll=2)

    def basis_copies(c):
        place = rows(c * 1024 + core * 512, 512)
        return (
            pltpu.make_async_copy(products.at[rows((core * 2 + c) * 512, 512)], basis_out.at[place], out_local.at[c]),
            pltpu.make_async_remote_copy(
                src_ref=products.at[rows(((1 - core) * 2 + c) * 512, 512)],
                dst_ref=basis_out.at[place],
                send_sem=out_send.at[c],
                recv_sem=out_recv.at[c],
                device_id=(half, point, 1 - core),
                device_id_type=MESH,
            ),
        )

    def residual_copies(c):
        place = rows(c * 32 + core * 16, 16)
        return (
            pltpu.make_async_copy(lanes.at[rows((core * 2 + c) * 16, 16)], residual_out.at[place], out_local.at[2 + c]),
            pltpu.make_async_remote_copy(
                src_ref=lanes.at[rows(((1 - core) * 2 + c) * 16, 16)],
                dst_ref=residual_out.at[place],
                send_sem=out_send.at[2 + c],
                recv_sem=out_recv.at[2 + c],
                device_id=(half, point, 1 - core),
                device_id_type=MESH,
            ),
        )

    for c in range(2):
        for copy in basis_copies(c):
            copy.start()

    for slot in range(6, 8):
        back_wait(slot)
    first_lane = lax.broadcasted_iota(jnp.int32, (64, 128), 1) < 64
    first_lane_s = lax.broadcasted_iota(jnp.int32, (16, 128), 1) < 64

    def residual_point(s, carry):
        left = []
        for c in range(2):
            left.append(
                jnp.concatenate(
                    [received[pl.ds((r * 64 + 32 * half) * 32 + c * 16 + s, 32, stride=32), :] for r in range(2)], axis=0
                )
            )
        left = halves(jnp.concatenate(left, axis=1))
        real = received[pl.ds(192 * 32 + s, 64, stride=32), :]
        imag = received[pl.ds(192 * 32 + 16 + s, 64, stride=32), :]
        real_turn = pltpu.roll(real, 64, 1)
        imag_turn = pltpu.roll(imag, 64, 1)
        mixed[pl.ds(0, 64, stride=2), :] = jnp.where(first_lane, real, imag_turn)
        mixed[pl.ds(1, 64, stride=2), :] = jnp.where(first_lane, real_turn, imag)
        mixed[pl.ds(128, 64, stride=2), :] = jnp.where(first_lane, -imag, real_turn)
        mixed[pl.ds(129, 64, stride=2), :] = jnp.where(first_lane, -imag_turn, real)
        right = halves(mixed[...])
        both = dot(jnp.concatenate(left, axis=0), right[0])
        pairs[rows(s * 64, 64), :] = both[:64] + both[64:] + dot(left[0], right[1])
        return carry

    lax.fori_loop(0, 16, residual_point, 0, unroll=2)

    for r in range(2):
        for k in range(16):
            even = pairs[pl.ds(r * 32 + 2 * k, 16, stride=64), :]
            odd = pairs[pl.ds(r * 32 + 2 * k + 1, 16, stride=64), :]
            lanes[pl.ds((r * 2) * 16, 16), k * 128 : (k + 1) * 128] = jnp.where(first_lane_s, even, pltpu.roll(odd, 64, 1))
            lanes[pl.ds((r * 2 + 1) * 16, 16), k * 128 : (k + 1) * 128] = jnp.where(first_lane_s, pltpu.roll(even, 64, 1), odd)

    for c in range(2):
        for copy in residual_copies(c):
            copy.start()
    for c in range(2):
        for copy in basis_copies(c) + residual_copies(c):
            copy.wait()


def per_device(children, residual_series):
    outer, inner = transform_matrices()
    hbm = pl.BlockSpec(memory_space=pltpu.HBM)
    basis, residual = pl.pallas_call(
        kernel,
        name="merge",
        out_shape=(
            jax.ShapeDtypeStruct((2 * WITHIN * 32, 128), F32),
            jax.ShapeDtypeStruct((2 * WITHIN, 2048), F32),
        ),
        in_specs=[hbm] * 4,
        out_specs=(hbm, hbm),
        scratch_shapes=[
            pltpu.VMEM((WITHIN * 64, 128), F32),
            pltpu.VMEM((WITHIN, 2048), F32),
            pltpu.VMEM((RING * WAVES * SLAB, 128), F32),
            pltpu.VMEM((WAVES * SLAB, 128), F32),
            pltpu.VMEM((2 * WITHIN * PLANE, 128), F32),
            pltpu.VMEM((8 * 1024, 128), F32),
            pltpu.VMEM((256 * 32, 128), F32),
            pltpu.VMEM((4 * 512, 128), F32),
            pltpu.VMEM((16 * 64, 128), F32),
            pltpu.VMEM((256, 128), F32),
            pltpu.VMEM((64, 2048), F32),
            pltpu.VMEM((32, 256), BF16),
            pltpu.VMEM((PLANE * 64, 256), BF16),
            pltpu.SemaphoreType.DMA((WAVES,)),
            pltpu.SemaphoreType.DMA((WAVES,)),
            pltpu.SemaphoreType.DMA((WAVES + 8,)),
            pltpu.SemaphoreType.DMA((WAVES * PARTS * 2 * HOPS,)),
            pltpu.SemaphoreType.DMA((WAVES * PARTS * 2 * HOPS,)),
            pltpu.SemaphoreType.DMA((8,)),
            pltpu.SemaphoreType.DMA((8,)),
            pltpu.SemaphoreType.DMA((4,)),
            pltpu.SemaphoreType.DMA((4,)),
            pltpu.SemaphoreType.DMA((4,)),
            pltpu.SemaphoreType.DMA((4,)),
        ],
        compiler_params=pltpu.CompilerParams(collective_id=0, has_side_effects=True, vmem_limit_bytes=62 * 2**20),
    )(
        children.reshape(WITHIN * 64, 128),
        residual_series,
        jnp.asarray(outer),
        jnp.asarray(inner),
    )
    return basis.reshape(2, WITHIN, 32, 128), residual.reshape(2, WITHIN, 2048)


def solution(mesh):
    placed = (P("half", "point", "row", None), P("point", ("row", "half")))
    return jax.shard_map(
        per_device,
        mesh=mesh,
        in_specs=placed,
        out_specs=(P(None, "point", ("row", "half"), None), P(None, "point", ("row", "half"))),
        check_vma=False,
    )
```

```python
import math

import jax
import jax.numpy as jnp
import numpy as np
from jax import lax
from jax.experimental import pallas as pl
from jax.experimental.pallas import tpu as pltpu
from jax.sharding import PartitionSpec as P

BASIS = 128
BLOCK = 64
LENGTH = 524288
WITHIN = 32
GROUPS = 64
PLANE = 16
RING = 8
WAVES = 5
HOPS = 5
PARTS = 2
SLAB = PLANE * WITHIN
PART = SLAB // PARTS
STARTS = {'L0': 0, 'L1': 1, 'L2': 5, 'L3': 3, 'U0': 0, 'U1': 3, 'S0': 8, 'S1': 8}
LEAD = 0
MESH = pl.DeviceIdType.MESH
F32 = jnp.float32
BF16 = jnp.bfloat16


def split_matrix(matrix):
    matrix = matrix.astype(np.float32)
    high = matrix.astype(jnp.bfloat16)
    low = (matrix - high.astype(np.float32)).astype(jnp.bfloat16)
    return np.concatenate([high, high, low, low], axis=-1)


def transform_matrices():
    q = np.arange(GROUPS).reshape(4, PLANE)
    p = np.arange(GROUPS)
    phase = (32 * p[None, None, :] * (256 * q[:, :, None] + 1)) % LENGTH
    angle = phase * (2.0 * math.pi / LENGTH)
    outer = np.concatenate([np.cos(angle), np.sin(angle)], axis=1)
    t = np.arange(WITHIN)
    s = np.arange(WITHIN)
    phase = t[None, None, None, :] * (s[None, None, :, None] * 16384 + 256 * q[:, :, None, None] + 1)
    angle = (phase % LENGTH) * (2.0 * math.pi / LENGTH)
    cos, sin = np.cos(angle), np.sin(angle)
    real = np.concatenate([cos, -sin], axis=-1).reshape(4, PLANE, 2, 1, 16, 64)
    imag = np.concatenate([sin, cos], axis=-1).reshape(4, PLANE, 2, 1, 16, 64)
    inner = np.concatenate([real, imag], axis=3).reshape(4, PLANE * 64, 64)
    return split_matrix(outer), split_matrix(inner)


def halves(x):
    high = x.astype(BF16)
    return high, (x - high.astype(F32)).astype(BF16)


def stacked_halves(x):
    high, low = halves(x)
    return jnp.concatenate([high, low, high, low], axis=0)


def dot(a, b):
    return jnp.dot(a, b, preferred_element_type=F32)


def rows(offset, count):
    return pl.ds(pl.multiple_of(offset, 8), count)


def parts_of(item):
    return range(2 * PARTS if item[0] == "U" else PARTS)


def waves_of(item):
    kind, number = item[0], int(item[1])
    return {"L": [number], "U": [2 * number, 2 * number + 1], "S": [4]}[kind]


def reach(item, source, direction, part):
    in_lower = source < 4
    if item[0] == "L":
        return jnp.where(in_lower, source + 2 if direction == 0 else 5 - source, 0)
    if item[0] == "S":
        hops = 4 if (direction == 0) == (part < PARTS // 2) else 3
        return jnp.where(in_lower if item == "S0" else source >= 4, hops, 0)
    if part % 2 == 1:
        hops = 7 - source if direction == 0 else source - 4
    elif direction == 0:
        hops = jnp.where(source >= 6, 11 - source, 0)
    else:
        hops = jnp.where(source <= 5, source, 0)
    return jnp.where(in_lower, 0, hops)


def longest(item, direction, part):
    if item[0] == "S":
        return 4 if (direction == 0) == (part < PARTS // 2) else 3
    if item[0] == "U" and part % 2 == 1:
        return 3
    return 5


def kernel(
    child_in, series_in, outer_all, inner_all, basis_out, residual_out,
    child, series, gathered, sending, mid, spectra, received, products, pairs, mixed, lanes, outer, inner,
    a_send, a_recv, own_sem, z_send, z_recv, d_send, d_recv, const_sem, out_local, out_send, out_recv,
):
    half = lax.axis_index("half")
    point = lax.axis_index("point")
    core = lax.axis_index("row")
    z = point // 16
    plane = point % 16
    y = plane // 4
    x = plane % 4
    ring = half * 4 + z

    def plane_peer(i):
        dy, dx = (i // 4) % 4, i % 4
        return ((y + dy) % 4) * 4 + (x + dx) % 4

    def ring_device(position):
        return (position // 4, (position % 4) * 16 + plane, core)

    consts = [
        pltpu.make_async_copy(outer_all.at[z], outer, const_sem.at[0]),
        pltpu.make_async_copy(inner_all.at[z], inner, const_sem.at[1]),
    ]
    loads = [
        pltpu.make_async_copy(child_in, child, const_sem.at[2]),
        pltpu.make_async_copy(series_in, series, const_sem.at[3]),
    ]
    for copy in loads + consts:
        copy.start()

    barrier = pltpu.get_barrier_semaphore()

    def greet(i, carry):
        peer = plane_peer(i)
        pl.semaphore_signal(barrier, inc=1, device_id=(half, z * 16 + peer, (core + i // 16) % 2), device_id_type=MESH)
        return carry

    lax.fori_loop(1, 32, greet, 0)
    for step in (1, 7):
        pl.semaphore_signal(barrier, inc=1, device_id=ring_device((ring + step) % 8), device_id_type=MESH)

    for wave in range(WAVES):
        if wave in (0, 4):
            loads[wave // 4].wait()
        for m in range(PLANE):
            base = (wave * PLANE + m) * WITHIN
            if wave < 4:
                row = (wave % 2) * 32 + 2 * m + wave // 2
                sending[pl.ds(base, WITHIN), :] = child[pl.ds(row, WITHIN, stride=64), :]
            else:
                sending[pl.ds(base, WITHIN), :] = series[:, m * 128 : (m + 1) * 128]
    pl.semaphore_wait(barrier, 33)

    def slab(source, wave):
        return (source * WAVES + wave) * SLAB

    def spread(wave):
        own = slab(ring, wave) + plane * WITHIN

        def send(i, carry):
            peer = plane_peer(i)
            pltpu.make_async_remote_copy(
                src_ref=sending.at[rows((wave * PLANE + peer) * WITHIN, WITHIN)],
                dst_ref=gathered.at[rows(own, WITHIN)],
                send_sem=a_send.at[wave],
                recv_sem=a_recv.at[wave],
                device_id=(half, z * 16 + peer, core),
                device_id_type=MESH,
            ).start()
            return carry

        lax.fori_loop(1, PLANE, send, 0)
        pltpu.make_async_copy(
            sending.at[rows((wave * PLANE + plane) * WITHIN, WITHIN)], gathered.at[rows(own, WITHIN)], own_sem.at[wave]
        ).start()

    def spread_wait(wave):
        own = slab(ring, wave)
        count = (PLANE - 1) * WITHIN
        pltpu.make_async_remote_copy(
            src_ref=sending.at[pl.ds(wave * SLAB, count)],
            dst_ref=gathered.at[rows(own, count)],
            send_sem=a_send.at[wave],
            recv_sem=a_recv.at[wave],
            device_id=(half, point, 1 - core),
            device_id_type=MESH,
        ).wait()
        pltpu.make_async_copy(
            sending.at[pl.ds(0, WITHIN)], gathered.at[rows(own, WITHIN)], own_sem.at[wave]
        ).wait()

    def ring_copy(item, direction, hop, part, source):
        number = int(item[1])
        if item[0] == "U":
            offset = slab(source, 2 * number + part % 2) + part // 2 * PART
            stream = 2 * number * PARTS + part
        else:
            wave = waves_of(item)[0]
            offset = slab(source, wave) + part * PART
            stream = wave * PARTS + part
        place = rows(offset, PART)
        index = (stream * 2 + direction) * HOPS + hop
        return pltpu.make_async_remote_copy(
            src_ref=gathered.at[place],
            dst_ref=gathered.at[place],
            send_sem=z_send.at[index],
            recv_sem=z_recv.at[index],
            device_id=ring_device((ring + (1 if direction == 0 else 7)) % 8),
            device_id_type=MESH,
        )

    def origin(direction, hop):
        return (ring + (8 - hop if direction == 0 else hop)) % 8

    def begin(item):
        for part in parts_of(item):
            for direction in range(2):

                @pl.when(reach(item, ring, direction, part) >= 1)
                def _():
                    ring_copy(item, direction, 0, part, ring).start()

    def relay(item, hop):
        for part in parts_of(item):
            for direction in range(2):
                if longest(item, direction, part) < hop:
                    continue
                source = origin(direction, hop)
                extent = reach(item, source, direction, part)

                @pl.when(extent >= hop)
                def _():
                    ring_copy(item, direction, hop - 1, part, source).wait_recv()
                    if longest(item, direction, part) > hop:

                        @pl.when(extent > hop)
                        def _():
                            ring_copy(item, direction, hop, part, source).start()

    def ring_finish():
        for item in STARTS:
            for part in parts_of(item):
                for direction in range(2):
                    for hop in range(longest(item, direction, part)):
                        source = origin(direction, hop)

                        @pl.when(reach(item, source, direction, part) > hop)
                        def _():
                            ring_copy(item, direction, hop, part, source).wait_send()

    def transform(first, wave, slot, place):
        def over_t(step, carry):
            columns = []
            for k in range(2):
                t = step * 2 + k
                column = jnp.concatenate(
                    [gathered[pl.ds(slab(first + i, wave) + t, PLANE, stride=WITHIN), :] for i in range(4)], axis=0
                )
                columns.append(stacked_halves(column))
            out = dot(outer[...], jnp.concatenate(columns, axis=1))
            for k in range(2):
                t = step * 2 + k
                mid[rows(t * PLANE, PLANE), :] = out[:PLANE, k * 128 : (k + 1) * 128]
                mid[rows((WITHIN + t) * PLANE, PLANE), :] = out[PLANE:, k * 128 : (k + 1) * 128]
            return carry

        lax.fori_loop(0, WITHIN // 2, over_t, 0, unroll=16)

        def over_q(q, carry):
            values = mid[pl.ds(q, 2 * WITHIN, stride=PLANE), :]
            out = dot(inner[rows(q * 64, 64), :], stacked_halves(values))
            spectra[rows(slot * 1024 + q * 64, 64), :] = out
            return carry

        lax.fori_loop(0, PLANE, over_q, 0, unroll=16)

        def back(i, carry):
            peer = plane_peer(i)
            other = (core + i // 16) % 2
            pltpu.make_async_remote_copy(
                src_ref=spectra.at[rows(slot * 1024 + peer * 64 + other * 32, 32)],
                dst_ref=received.at[rows(place * 32, 32)],
                send_sem=d_send.at[slot],
                recv_sem=d_recv.at[slot],
                device_id=(half, z * 16 + peer, other),
                device_id_type=MESH,
            ).start()
            return carry

        lax.fori_loop(1, 32, back, 0, unroll=4)
        pltpu.make_async_copy(
            spectra.at[rows(slot * 1024 + plane * 64 + core * 32, 32)], received.at[rows(place * 32, 32)], own_sem.at[WAVES + slot]
        ).start()

    def back_wait(slot):
        pltpu.make_async_remote_copy(
            src_ref=spectra.at[pl.ds(slot * 1024, 31 * 32)],
            dst_ref=received.at[pl.ds(0, 31 * 32)],
            send_sem=d_send.at[slot],
            recv_sem=d_recv.at[slot],
            device_id=(half, point, 1 - core),
            device_id_type=MESH,
        ).wait()
        pltpu.make_async_copy(
            spectra.at[pl.ds(0, 32)], received.at[pl.ds(0, 32)], own_sem.at[WAVES + slot]
        ).wait()

    for wave in range(WAVES):
        spread(wave)

    events = []
    for item, start in STARTS.items():
        last = 4 if item[0] == "S" else HOPS
        events.append((start - LEAD, 1, start, item, 0))
        events += [(start + hop, 0, start, item, hop) for hop in range(1, last + 1)]
        events.append((start + last, 2, start, item, 0))
    ready = set()
    ready_consts = False
    for _, kind, _, item, hop in sorted(events):
        number = int(item[1])
        if kind == 0:
            relay(item, hop)
        elif kind == 1:
            for wave in waves_of(item):
                if wave not in ready:
                    spread_wait(wave)
                    ready.add(wave)
            begin(item)
        else:
            if not ready_consts:
                for copy in consts:
                    copy.wait()
                ready_consts = True
            if item[0] == "L":
                transform(0, number, number, core * 64 + number % 2 * 32 + 2 * plane + number // 2)
            elif item[0] == "U":
                transform(4, 2 * number + half, 4 + number, 128 + core * 32 + 2 * plane + number)
            else:
                transform(4 * number, 4, 6 + number, 192 + core * 32 + number * 16 + plane)

    ring_finish()
    for slot in range(6):
        back_wait(slot)

    def basis_point(s, carry):
        lower = [halves(received[pl.ds(c * 16 + s, 128, stride=32), :]) for c in range(2)]
        upper = [halves(received[pl.ds(128 * 32 + c * 16 + s, 64, stride=32), :]) for c in range(2)]
        right = [
            jnp.concatenate(
                [
                    jnp.concatenate([lower[0][k], lower[1][k]], axis=1),
                    jnp.concatenate([-lower[1][k], lower[0][k]], axis=1),
                ],
                axis=0,
            )
            for k in range(2)
        ]
        left = [jnp.concatenate([upper[0][k], upper[1][k]], axis=1) for k in range(2)]
        both = dot(jnp.concatenate(left, axis=0), right[0])
        out = both[:64] + both[64:] + dot(left[0], right[1])
        for r in range(2):
            for c in range(2):
                products[rows(((r * 2 + c) * 16 + s) * 32, 32), :] = out[r * 32 : (r + 1) * 32, c * 128 : (c + 1) * 128]
        return carry

    lax.fori_loop(0, 16, basis_point, 0, unroll=2)

    def basis_copies(c):
        place = rows(c * 1024 + core * 512, 512)
        return (
            pltpu.make_async_copy(products.at[rows((core * 2 + c) * 512, 512)], basis_out.at[place], out_local.at[c]),
            pltpu.make_async_remote_copy(
                src_ref=products.at[rows(((1 - core) * 2 + c) * 512, 512)],
                dst_ref=basis_out.at[place],
                send_sem=out_send.at[c],
                recv_sem=out_recv.at[c],
                device_id=(half, point, 1 - core),
                device_id_type=MESH,
            ),
        )

    def residual_copies(c):
        place = rows(c * 32 + core * 16, 16)
        return (
            pltpu.make_async_copy(lanes.at[rows((core * 2 + c) * 16, 16)], residual_out.at[place], out_local.at[2 + c]),
            pltpu.make_async_remote_copy(
                src_ref=lanes.at[rows(((1 - core) * 2 + c) * 16, 16)],
                dst_ref=residual_out.at[place],
                send_sem=out_send.at[2 + c],
                recv_sem=out_recv.at[2 + c],
                device_id=(half, point, 1 - core),
                device_id_type=MESH,
            ),
        )

    for c in range(2):
        for copy in basis_copies(c):
            copy.start()

    for slot in range(6, 8):
        back_wait(slot)
    first_lane = lax.broadcasted_iota(jnp.int32, (64, 128), 1) < 64
    first_lane_s = lax.broadcasted_iota(jnp.int32, (16, 128), 1) < 64

    def residual_point(s, carry):
        left = []
        for c in range(2):
            left.append(
                jnp.concatenate(
                    [received[pl.ds((r * 64 + 32 * half) * 32 + c * 16 + s, 32, stride=32), :] for r in range(2)], axis=0
                )
            )
        left = halves(jnp.concatenate(left, axis=1))
        real = received[pl.ds(192 * 32 + s, 64, stride=32), :]
        imag = received[pl.ds(192 * 32 + 16 + s, 64, stride=32), :]
        real_turn = pltpu.roll(real, 64, 1)
        imag_turn = pltpu.roll(imag, 64, 1)
        mixed[pl.ds(0, 64, stride=2), :] = jnp.where(first_lane, real, imag_turn)
        mixed[pl.ds(1, 64, stride=2), :] = jnp.where(first_lane, real_turn, imag)
        mixed[pl.ds(128, 64, stride=2), :] = jnp.where(first_lane, -imag, real_turn)
        mixed[pl.ds(129, 64, stride=2), :] = jnp.where(first_lane, -imag_turn, real)
        right = halves(mixed[...])
        both = dot(jnp.concatenate(left, axis=0), right[0])
        pairs[rows(s * 64, 64), :] = both[:64] + both[64:] + dot(left[0], right[1])
        return carry

    lax.fori_loop(0, 16, residual_point, 0, unroll=2)

    for r in range(2):
        for k in range(16):
            even = pairs[pl.ds(r * 32 + 2 * k, 16, stride=64), :]
            odd = pairs[pl.ds(r * 32 + 2 * k + 1, 16, stride=64), :]
            lanes[pl.ds((r * 2) * 16, 16), k * 128 : (k + 1) * 128] = jnp.where(first_lane_s, even, pltpu.roll(odd, 64, 1))
            lanes[pl.ds((r * 2 + 1) * 16, 16), k * 128 : (k + 1) * 128] = jnp.where(first_lane_s, pltpu.roll(even, 64, 1), odd)

    for c in range(2):
        for copy in residual_copies(c):
            copy.start()
    for c in range(2):
        for copy in basis_copies(c) + residual_copies(c):
            copy.wait()


def per_device(children, residual_series):
    outer, inner = transform_matrices()
    hbm = pl.BlockSpec(memory_space=pltpu.HBM)
    basis, residual = pl.pallas_call(
        kernel,
        name="merge",
        out_shape=(
            jax.ShapeDtypeStruct((2 * WITHIN * 32, 128), F32),
            jax.ShapeDtypeStruct((2 * WITHIN, 2048), F32),
        ),
        in_specs=[hbm] * 4,
        out_specs=(hbm, hbm),
        scratch_shapes=[
            pltpu.VMEM((WITHIN * 64, 128), F32),
            pltpu.VMEM((WITHIN, 2048), F32),
            pltpu.VMEM((RING * WAVES * SLAB, 128), F32),
            pltpu.VMEM((WAVES * SLAB, 128), F32),
            pltpu.VMEM((2 * WITHIN * PLANE, 128), F32),
            pltpu.VMEM((8 * 1024, 128), F32),
            pltpu.VMEM((256 * 32, 128), F32),
            pltpu.VMEM((4 * 512, 128), F32),
            pltpu.VMEM((16 * 64, 128), F32),
            pltpu.VMEM((256, 128), F32),
            pltpu.VMEM((64, 2048), F32),
            pltpu.VMEM((32, 256), BF16),
            pltpu.VMEM((PLANE * 64, 256), BF16),
            pltpu.SemaphoreType.DMA((WAVES,)),
            pltpu.SemaphoreType.DMA((WAVES,)),
            pltpu.SemaphoreType.DMA((WAVES + 8,)),
            pltpu.SemaphoreType.DMA((WAVES * PARTS * 2 * HOPS,)),
            pltpu.SemaphoreType.DMA((WAVES * PARTS * 2 * HOPS,)),
            pltpu.SemaphoreType.DMA((8,)),
            pltpu.SemaphoreType.DMA((8,)),
            pltpu.SemaphoreType.DMA((4,)),
            pltpu.SemaphoreType.DMA((4,)),
            pltpu.SemaphoreType.DMA((4,)),
            pltpu.SemaphoreType.DMA((4,)),
        ],
        compiler_params=pltpu.CompilerParams(collective_id=0, has_side_effects=True, vmem_limit_bytes=62 * 2**20),
    )(
        children.reshape(WITHIN * 64, 128),
        residual_series,
        jnp.asarray(outer),
        jnp.asarray(inner),
    )
    return basis.reshape(2, WITHIN, 32, 128), residual.reshape(2, WITHIN, 2048)


def solution(mesh):
    placed = (P("half", "point", "row", None), P("point", ("row", "half")))
    return jax.shard_map(
        per_device,
        mesh=mesh,
        in_specs=placed,
        out_specs=(P(None, "point", ("row", "half"), None), P(None, "point", ("row", "half"))),
        check_vma=False,
    )
```
